32 devices in a mesh: dp: 2 (over y), section: 4 (over x, core), tensor: 4 (over z).
Axes of the slice: x: 2, y: 2, z: 4, core: 2. Of those that a mesh axis runs over, the one named last changes fastest.
Arguments:
- sent_cot: bfloat16 [2, 4, 2, 56, 8192], P('dp', 'section', None, 'tensor'), may hold values from -6 to 6
- saved_heads: bfloat16 [2, 4, 2, 56, 1024], P('dp', 'section', None, None, 'tensor'), may hold values from -0.29882812 to 0.29882812
- out_proj: bfloat16 [4, 8192, 1024], P('section', None, 'tensor'), may hold values from -0.0625 to 0.0625
Outputs:
- head_grads: bfloat16 [2, 4, 2, 56, 1024], P('dp', 'section', None, None, 'tensor')
- proj_grad: bfloat16 [4, 8192, 1024], P('section', 'dp', 'tensor')
The draws below stay inside these ranges and needn't reach their ends.
All inputs are finite; a program needn't handle non-finite values.
Results may differ from the reference program's by a relative error of at most 0.013.
Values may be sent and summed in bfloat16 or wider, within the bound.
A program may use at most 64 MiB of HBM per device.

```python
import jax
import jax.numpy as jnp
from jax import lax

D = 8192
HD_ALL = 1024
GROUP = 56
SECTIONS = 4
N_DP = 2


def block_levels(own_key, shape, shards, least, top_value):
    loudness = 1.0
    for position, parts in shards:
        draws = jax.random.uniform(jax.random.fold_in(jax.random.fold_in(own_key, 6), position), (parts,), jnp.float32, least / len(shards), top_value / len(shards))
        loudness = loudness * jnp.repeat(jnp.exp(draws), shape[position] // parts).reshape((-1,) + (1,) * (len(shape) - 1 - position))
    return loudness


def bell_draw(own_key, extent, spread, limit, shards=(), dtype=jnp.bfloat16):
    array = spread * jax.random.normal(own_key, extent, jnp.float32)
    if shards:
        array = array * block_levels(own_key, extent, shards, -0.22, 0.18)
    return jnp.clip(array, -limit, limit).astype(dtype)


def setup_inputs(seed: int = 0) -> dict:
    key_of = jax.random.split(jax.random.key(seed), 4)
    return {
        "sent_cot": bell_draw(key_of[0], (N_DP, SECTIONS, 2, GROUP, D), 1.0, 6.0, ((0, 2), (1, 4), (3, 4))),
        "saved_heads": bell_draw(key_of[1], (N_DP, SECTIONS, 2, GROUP, HD_ALL), 0.05, 0.29882812, ((0, 2), (1, 4), (4, 4))),
        "out_proj": bell_draw(key_of[2], (SECTIONS, D, HD_ALL), D ** -0.5, 0.0625, ((0, 4), (2, 4))),
    }


def section_grads(operands):
    incoming, head_rows, weight = operands
    width = incoming.shape[-1]
    flat_rows = incoming.reshape(-1, width)
    head_grads = jnp.dot(flat_rows, weight, preferred_element_type=jnp.float32)
    head_grads = head_grads.astype(jnp.bfloat16).reshape(head_rows.shape)
    proj_total = jnp.zeros(weight.shape, jnp.float32)
    for member in range(incoming.shape[0]):
        grad_rows = incoming[member].reshape(-1, width)
        act_rows = head_rows[member].reshape(-1, head_rows.shape[-1])
        group_term = jnp.dot(grad_rows.T, act_rows, preferred_element_type=jnp.float32).astype(jnp.bfloat16)
        group_term = lax.optimization_barrier(group_term)
        proj_total = proj_total + group_term.astype(jnp.float32)
    return head_grads, proj_total.astype(jnp.bfloat16)


def reference(sent_cot, saved_heads, out_proj):
    from_above = jnp.roll(sent_cot[:, :, 0], -1, axis=1)
    from_below = jnp.roll(sent_cot[:, :, 1], 1, axis=1)
    incoming = jnp.stack([from_above, from_below], axis=2)
    head_grads, proj_grad = lax.map(section_grads, (jnp.swapaxes(incoming, 0, 1), jnp.swapaxes(saved_heads, 0, 1), out_proj))
    return jnp.swapaxes(head_grads, 0, 1), proj_grad
```

```python
import functools

import jax
import jax.numpy as jnp
from jax import lax
from jax.experimental import pallas as pl
from jax.experimental.pallas import tpu as pltpu
from jax.sharding import PartitionSpec as P

MESH = pl.DeviceIdType.MESH
F32 = jnp.float32
ROWS = 16


def kernel(dims, packed, heads, weight, head_out, proj_out,
           gath, hbuf, hfull, hspare, wbuf, stage, acc, spare, acc_in, hstage,
           s1, r1, s2, r2, hs, hr, xs, xr, loc, outs):
    n_dp, n_sec, n_ten, tiles, width, tokens, parts = dims
    dp, sec, ten = (lax.axis_index(a) for a in ("dp", "section", "tensor"))
    spots = [(0, lax.rem(sec + n_sec - 1, n_sec)), (1, lax.rem(sec + 1, n_sec))]
    others = [lax.rem(dp + k, n_dp) for k in range(1, n_dp)]
    has_left, has_right = ten > 0, ten < n_ten - 1

    own_heads = pltpu.make_async_copy(heads, hbuf.at[dp], loc.at[0])
    own_heads.start()
    rows = width * (tiles + 1)
    load = pltpu.make_async_copy(weight.at[pl.ds(pl.multiple_of(dp * rows, rows), rows)], wbuf, loc.at[1])
    load.start()

    barrier = pltpu.get_barrier_semaphore()
    for h in range(n_dp):
        for _, place in spots:
            pl.semaphore_signal(barrier, inc=1, device_id=(h, place, ten), device_id_type=MESH)
    for h in others:
        pl.semaphore_signal(barrier, inc=1, device_id=(h, sec, ten), device_id_type=MESH)

    @pl.when(has_left)
    def _():
        pl.semaphore_signal(barrier, inc=1, device_id=(dp, sec, ten - 1), device_id_type=MESH)

    @pl.when(has_right)
    def _():
        pl.semaphore_signal(barrier, inc=1, device_id=(dp, sec, ten + 1), device_id_type=MESH)

    pl.semaphore_wait(barrier, 2 * n_dp + n_dp - 1 + jnp.where(has_left, 1, 0) + jnp.where(has_right, 1, 0))

    def first(k, r, m):
        low, high = parts[m]
        h = lax.rem(dp + k, n_dp)
        cut = pl.ds(low, high - low)
        return pltpu.make_async_remote_copy(
            src_ref=packed.at[h, r, cut], dst_ref=gath.at[ten, dp, r, cut],
            send_sem=s1.at[k, r, m], recv_sem=r1.at[dp, r, m],
            device_id=(h, spots[r][1], ten), device_id_type=MESH)

    def first_arrival(g, r, m):
        low, high = parts[m]
        cut = pl.ds(low, high - low)
        return pltpu.make_async_remote_copy(
            src_ref=packed.at[0, r, cut], dst_ref=gath.at[ten, g, r, cut],
            send_sem=s1.at[0, r, m], recv_sem=r1.at[g, r, m],
            device_id=(dp, spots[r][1], ten), device_id_type=MESH)

    def hop(item, g, m, step):
        low, high = parts[m]
        block = gath.at[item, g, :, pl.ds(low, high - low)]
        return pltpu.make_async_remote_copy(
            src_ref=block, dst_ref=block,
            send_sem=s2.at[(step + 1) // 2, item, g, m], recv_sem=r2.at[item, g, m],
            device_id=(dp, sec, ten + step), device_id_type=MESH)

    for m in range(len(parts)):
        for k in range(n_dp):
            for r in range(2):
                first(k, r, m).start()
    own_heads.wait()

    def head_copy(k):
        return pltpu.make_async_remote_copy(
            src_ref=heads, dst_ref=hbuf.at[dp],
            send_sem=hs.at[k - 1], recv_sem=hr.at[dp],
            device_id=(lax.rem(dp + k, n_dp), sec, ten), device_id_type=MESH)

    for k in range(1, n_dp):
        head_copy(k).start()

    for m in range(len(parts)):
        for k in range(n_dp):
            g = lax.rem(dp + k, n_dp)
            for r in range(2):
                first_arrival(g, r, m).wait_recv()

            @pl.when(has_right)
            def _():
                hop(ten, g, m, 1).start()

            @pl.when(has_left)
            def _():
                hop(ten, g, m, -1).start()

    for g in others:
        pltpu.make_async_remote_copy(
            src_ref=heads, dst_ref=hbuf.at[g], send_sem=hs.at[0], recv_sem=hr.at[g],
            device_id=(g, sec, ten), device_id_type=MESH).wait_recv()
    load.wait()
    count = hbuf.shape[1]
    place = lax.rem(lax.broadcasted_iota(jnp.int32, (count, hbuf.shape[2]), 0), ROWS)
    extra = ROWS - tokens
    for g in range(n_dp):
        wide = hbuf[g].astype(F32)
        hfull[g] = jnp.where(place < tokens, wide, 0.0).astype(jnp.bfloat16)
        for c in range(tiles):
            turned = pltpu.roll(wide, tokens - extra * c, 0) if tokens - extra * c else wide
            hspare[g, c] = jnp.where(place >= tokens, turned, 0.0).astype(jnp.bfloat16)
        acc[g] = jnp.zeros(acc.shape[1:], F32)
        spare[g] = jnp.zeros(spare.shape[1:], F32)

    def out_copy(c):
        cut = pl.ds(c * width, width)
        return pltpu.make_async_copy(stage.at[cut], proj_out.at[cut], outs.at[c])

    def tile_products(c):
        total = None
        last_rows = wbuf[tiles * width:(tiles + 1) * width]
        for g in range(n_dp):
            block = gath[:, g, :, c].reshape(count, width)
            term = lax.dot_general(block, hfull[g], (((0,), (0,)), ((), ())), preferred_element_type=F32)
            term = term.astype(jnp.bfloat16).astype(F32)
            total = term if total is None else total + term
            spare[g] += lax.dot_general(block, hspare[g, c], (((0,), (0,)), ((), ())), preferred_element_type=F32)
            head = jnp.dot(block, wbuf[c * width:(c + 1) * width], preferred_element_type=F32)
            tail = jnp.dot(block, last_rows, preferred_element_type=F32)
            back = count - (tokens - extra * c)
            tail = pltpu.roll(tail, back, 0) if back != count else tail
            mine = (place >= extra * c) & (place < extra * (c + 1))
            acc[g] += head + jnp.where(mine, tail, 0.0)
        stage[c * width:(c + 1) * width] = total.astype(jnp.bfloat16)
        out_copy(c).start()

    def pass_on(d, m):
        for k in range(n_dp - 1, -1, -1):
            g = lax.rem(dp + k, n_dp)

            @pl.when(ten - d >= 0)
            def _():
                hop(ten - d, g, m, 1).wait_recv()

                @pl.when(has_right)
                def _():
                    hop(ten - d, g, m, 1).start()

            @pl.when(ten + d < n_ten)
            def _():
                hop(ten + d, g, m, -1).wait_recv()

                @pl.when(has_left)
                def _():
                    hop(ten + d, g, m, -1).start()

    def middle(d, carry):
        for m in range(len(parts)):
            pass_on(d, m)
        return carry

    lax.fori_loop(1, n_ten - 1, middle, 0)
    for m, (low, high) in enumerate(parts):
        pass_on(n_ten - 1, m)
        for c in range(low, high):
            tile_products(c)

    def swap(k):
        g = lax.rem(dp + k, n_dp)
        return pltpu.make_async_remote_copy(
            src_ref=acc.at[g], dst_ref=acc_in.at[dp],
            send_sem=xs.at[k - 1], recv_sem=xr.at[dp],
            device_id=(g, sec, ten), device_id_type=MESH)

    for k in range(1, n_dp):
        swap(k).start()
    total = None
    for g in range(n_dp):
        term = spare[g].astype(jnp.bfloat16).astype(F32)
        total = term if total is None else total + term
    stage[tiles * width:(tiles + 1) * width] = total.astype(jnp.bfloat16)
    out_copy(tiles).start()

    for m in range(len(parts)):
        for k in range(n_dp):
            for r in range(2):
                first(k, r, m).wait_send()
    for k in range(1, n_dp):
        head_copy(k).wait_send()

    def drain(item, carry):
        for m in range(len(parts)):
            for g in range(n_dp):
                @pl.when(has_right & (item <= ten))
                def _():
                    hop(item, g, m, 1).wait_send()

                @pl.when(has_left & (item >= ten))
                def _():
                    hop(item, g, m, -1).wait_send()
        return carry

    lax.fori_loop(0, n_ten, drain, 0)

    result = acc[dp]
    for g in others:
        pltpu.make_async_remote_copy(
            src_ref=acc.at[g], dst_ref=acc_in.at[g], send_sem=xs.at[0], recv_sem=xr.at[g],
            device_id=(g, sec, ten), device_id_type=MESH).wait_recv()
        result = result + acc_in[g]
    hstage[...] = result.astype(jnp.bfloat16)
    store = pltpu.make_async_copy(hstage, head_out, loc.at[2])
    store.start()
    for k in range(1, n_dp):
        swap(k).wait_send()
    for c in range(tiles + 1):
        out_copy(c).wait()
    store.wait()


def per_device(mesh, sent_cot, saved_heads, out_proj):
    n_dp, n_sec, n_ten = (mesh.shape[a] for a in ("dp", "section", "tensor"))
    cot, heads, weight = sent_cot[0, 0], saved_heads[0, 0], out_proj[0]
    tokens, depth = cot.shape[1:]
    feats = weight.shape[1]
    extra = ROWS - tokens
    tiles = tokens // extra
    width = depth // n_dp // (tiles + 1)
    cut = cot.reshape(2, tokens, n_dp, tiles + 1, width).transpose(2, 0, 3, 1, 4)
    packed = jnp.concatenate(
        [cut[:, :, :tiles], cut[:, :, tiles].reshape(n_dp, 2, tiles, extra, width)], axis=3)
    blocks = heads.reshape(2, n_ten, tokens, feats).transpose(1, 0, 2, 3)
    count = n_ten * 2 * ROWS
    blocks = jnp.pad(blocks, ((0, 0), (0, 0), (0, extra), (0, 0))).reshape(count, feats)
    parts = ((0, 2), (2, 4), (4, 6), (6, 7)) if tiles == 7 else tuple((c, c + 1) for c in range(tiles))
    n_parts = len(parts)
    dims = (n_dp, n_sec, n_ten, tiles, width, tokens, parts)
    rows = depth // n_dp
    dma = pltpu.SemaphoreType.DMA
    head_out, proj = pl.pallas_call(
        functools.partial(kernel, dims),
        out_shape=(jax.ShapeDtypeStruct((count, feats), jnp.bfloat16),
                   jax.ShapeDtypeStruct((rows, feats), jnp.bfloat16)),
        in_specs=[pl.BlockSpec(memory_space=pl.ANY)] * 3,
        out_specs=(pl.BlockSpec(memory_space=pl.ANY),) * 2,
        scratch_shapes=[
            pltpu.VMEM((n_ten, n_dp, 2, tiles, ROWS, width), jnp.bfloat16),
            pltpu.VMEM((n_dp, count, feats), jnp.bfloat16),
            pltpu.VMEM((n_dp, count, feats), jnp.bfloat16),
            pltpu.VMEM((n_dp, tiles, count, feats), jnp.bfloat16),
            pltpu.VMEM((rows, feats), jnp.bfloat16),
            pltpu.VMEM((rows, feats), jnp.bfloat16),
            pltpu.VMEM((n_dp, count, feats), F32),
            pltpu.VMEM((n_dp, width, feats), F32),
            pltpu.VMEM((n_dp, count, feats), F32),
            pltpu.VMEM((count, feats), jnp.bfloat16),
            dma((n_dp, 2, n_parts)), dma((n_dp, 2, n_parts)),
            dma((2, n_ten, n_dp, n_parts)), dma((n_ten, n_dp, n_parts)),
            dma((n_dp,)), dma((n_dp,)), dma((n_dp,)), dma((n_dp,)),
            dma((3,)), dma((tiles + 1,)),
        ],
        compiler_params=pltpu.CompilerParams(
            collective_id=0, has_side_effects=True, vmem_limit_bytes=48 * 2**20),
        name="relay_grads",
    )(packed, blocks, weight)
    head = head_out.reshape(n_ten, 2, ROWS, feats)[:, :, :tokens].transpose(1, 0, 2, 3)
    return head.reshape(1, 1, 2, n_ten * tokens, feats), proj[None]


def solution(mesh):
    return jax.shard_map(
        functools.partial(per_device, mesh),
        mesh=mesh,
        in_specs=(
            P("dp", "section", None, "tensor", None),
            P("dp", "section", None, None, "tensor"),
            P("section", None, "tensor"),
        ),
        out_specs=(P("dp", "section", None, None, "tensor"), P("section", "dp", "tensor")),
        check_vma=False,
    )
```

```python
import functools

import jax
import jax.numpy as jnp
from jax import lax
from jax.experimental import pallas as pl
from jax.experimental.pallas import tpu as pltpu
from jax.sharding import PartitionSpec as P

MESH = pl.DeviceIdType.MESH
F32 = jnp.float32
ROWS = 16


def kernel(dims, packed, heads, weight, head_out, proj_out,
           gath, hbuf, hwide, hfull, hspare, wbuf, stage, part, acc, spare, acc_in, hstage,
           s1, r1, s2, r2, hs, hr, xs, xr, loc, outs):
    n_dp, n_sec, n_ten, tiles, width, tokens, parts = dims
    dp, sec, ten = (lax.axis_index(a) for a in ("dp", "section", "tensor"))
    spots = [(0, lax.rem(sec + n_sec - 1, n_sec)), (1, lax.rem(sec + 1, n_sec))]
    others = [lax.rem(dp + k, n_dp) for k in range(1, n_dp)]
    has_left, has_right = ten > 0, ten < n_ten - 1

    barrier = pltpu.get_barrier_semaphore()
    for h in range(n_dp):
        for _, place in spots:
            pl.semaphore_signal(barrier, inc=1, device_id=(h, place, ten), device_id_type=MESH)
    for h in others:
        pl.semaphore_signal(barrier, inc=1, device_id=(h, sec, ten), device_id_type=MESH)

    @pl.when(has_left)
    def _():
        pl.semaphore_signal(barrier, inc=1, device_id=(dp, sec, ten - 1), device_id_type=MESH)

    @pl.when(has_right)
    def _():
        pl.semaphore_signal(barrier, inc=1, device_id=(dp, sec, ten + 1), device_id_type=MESH)

    own_heads = pltpu.make_async_copy(heads, hbuf.at[dp], loc.at[0])
    own_heads.start()
    rows = width * (tiles + 1)
    load = pltpu.make_async_copy(weight.at[pl.ds(pl.multiple_of(dp * rows, rows), rows)], wbuf, loc.at[1])
    load.start()

    pl.semaphore_wait(barrier, 2 * n_dp + n_dp - 1 + jnp.where(has_left, 1, 0) + jnp.where(has_right, 1, 0))

    def first(k, r, m):
        low, high = parts[m]
        h = lax.rem(dp + k, n_dp)
        cut = pl.ds(low, high - low)
        return pltpu.make_async_remote_copy(
            src_ref=packed.at[h, r, cut], dst_ref=gath.at[ten, dp, r, cut],
            send_sem=s1.at[k, r, m], recv_sem=r1.at[dp, r, m],
            device_id=(h, spots[r][1], ten), device_id_type=MESH)

    def first_arrival(g, r, m):
        low, high = parts[m]
        cut = pl.ds(low, high - low)
        return pltpu.make_async_remote_copy(
            src_ref=packed.at[0, r, cut], dst_ref=gath.at[ten, g, r, cut],
            send_sem=s1.at[0, r, m], recv_sem=r1.at[g, r, m],
            device_id=(dp, spots[r][1], ten), device_id_type=MESH)

    def hop(item, g, m, step):
        low, high = parts[m]
        block = gath.at[item, g, :, pl.ds(low, high - low)]
        return pltpu.make_async_remote_copy(
            src_ref=block, dst_ref=block,
            send_sem=s2.at[(step + 1) // 2, item, g, m], recv_sem=r2.at[item, g, m],
            device_id=(dp, sec, ten + step), device_id_type=MESH)

    for m in range(len(parts)):
        for k in range(n_dp):
            for r in range(2):
                first(k, r, m).start()
    own_heads.wait()

    def head_copy(k):
        return pltpu.make_async_remote_copy(
            src_ref=heads, dst_ref=hbuf.at[dp],
            send_sem=hs.at[k - 1], recv_sem=hr.at[dp],
            device_id=(lax.rem(dp + k, n_dp), sec, ten), device_id_type=MESH)

    for k in range(1, n_dp):
        head_copy(k).start()

    for m in range(len(parts)):
        for k in range(n_dp):
            g = lax.rem(dp + k, n_dp)
            for r in range(2):
                first_arrival(g, r, m).wait_recv()

            @pl.when(has_right)
            def _():
                hop(ten, g, m, 1).start()

            @pl.when(has_left)
            def _():
                hop(ten, g, m, -1).start()

    for g in others:
        pltpu.make_async_remote_copy(
            src_ref=heads, dst_ref=hbuf.at[g], send_sem=hs.at[0], recv_sem=hr.at[g],
            device_id=(g, sec, ten), device_id_type=MESH).wait_recv()
    load.wait()
    count, feats = hwide.shape
    place = lax.rem(lax.broadcasted_iota(jnp.int32, (count, feats), 0), ROWS)
    length = n_ten * tokens
    extra = ROWS - tokens
    for g in range(n_dp):
        for r in range(2):
            lines = hbuf[g, r].astype(F32)
            for t in range(n_ten):
                turned = pltpu.roll(lines, length - t * tokens, 0) if t else lines
                at = (2 * t + r) * ROWS
                hwide[at:at + ROWS] = turned[:ROWS]
        wide = hwide[...]
        hfull[g] = jnp.where(place < tokens, wide, 0.0).astype(jnp.bfloat16)
        for c in range(tiles):
            turned = pltpu.roll(wide, tokens - extra * c, 0) if tokens - extra * c else wide
            hspare[g, c] = jnp.where(place >= tokens, turned, 0.0).astype(jnp.bfloat16)
        acc[g] = jnp.zeros(acc.shape[1:], F32)
        spare[g] = jnp.zeros(spare.shape[1:], F32)

    def out_copy(c):
        cut = pl.ds(c * width, width)
        return pltpu.make_async_copy(stage.at[cut], proj_out.at[cut], outs.at[c])

    def tile_term(g, c):
        block = gath[:, g, :, c].reshape(count, width)
        term = lax.dot_general(block, hfull[g], (((0,), (0,)), ((), ())), preferred_element_type=F32)
        spare[g] += lax.dot_general(block, hspare[g, c], (((0,), (0,)), ((), ())), preferred_element_type=F32)
        head = jnp.dot(block, wbuf[c * width:(c + 1) * width], preferred_element_type=F32)
        tail = jnp.dot(block, wbuf[tiles * width:(tiles + 1) * width], preferred_element_type=F32)
        back = count - (tokens - extra * c)
        tail = pltpu.roll(tail, back, 0) if back != count else tail
        mine = (place >= extra * c) & (place < extra * (c + 1))
        acc[g] += head + jnp.where(mine, tail, 0.0)
        return term.astype(jnp.bfloat16).astype(F32)

    def sum_others(terms):
        return functools.reduce(lambda a, b: a + b, terms)

    def pass_on(d, g, m):
        @pl.when(ten - d >= 0)
        def _():
            hop(ten - d, g, m, 1).wait_recv()

            @pl.when(has_right)
            def _():
                hop(ten - d, g, m, 1).start()

        @pl.when(ten + d < n_ten)
        def _():
            hop(ten + d, g, m, -1).wait_recv()

            @pl.when(has_left)
            def _():
                hop(ten + d, g, m, -1).start()

    def swap(k):
        g = lax.rem(dp + k, n_dp)
        return pltpu.make_async_remote_copy(
            src_ref=acc.at[g], dst_ref=acc_in.at[dp],
            send_sem=xs.at[k - 1], recv_sem=xr.at[dp],
            device_id=(g, sec, ten), device_id_type=MESH)

    def middle(d, carry):
        for g in others + [dp]:
            for m in range(len(parts)):
                pass_on(d, g, m)
        return carry

    lax.fori_loop(1, n_ten - 1, middle, 0)
    for m, (low, high) in enumerate(parts):
        for g in others:
            pass_on(n_ten - 1, g, m)
        for c in range(low, high):
            part[c * width:(c + 1) * width] = sum_others([tile_term(g, c) for g in others])
    for k in range(1, n_dp):
        swap(k).start()
    part[tiles * width:] = sum_others([spare[g].astype(jnp.bfloat16).astype(F32) for g in others])
    for m, (low, high) in enumerate(parts):
        pass_on(n_ten - 1, dp, m)
        for c in range(low, high):
            cut = slice(c * width, (c + 1) * width)
            stage[cut] = (part[cut] + tile_term(dp, c)).astype(jnp.bfloat16)
            out_copy(c).start()

    own = spare[dp].astype(jnp.bfloat16).astype(F32)
    stage[tiles * width:] = (part[tiles * width:] + own).astype(jnp.bfloat16)
    out_copy(tiles).start()

    for m in range(len(parts)):
        for k in range(n_dp):
            for r in range(2):
                first(k, r, m).wait_send()
    for k in range(1, n_dp):
        head_copy(k).wait_send()

    def drain(item, carry):
        for m in range(len(parts)):
            for g in range(n_dp):
                @pl.when(has_right & (item <= ten))
                def _():
                    hop(item, g, m, 1).wait_send()

                @pl.when(has_left & (item >= ten))
                def _():
                    hop(item, g, m, -1).wait_send()
        return carry

    lax.fori_loop(0, n_ten, drain, 0)

    result = acc[dp]
    for g in others:
        pltpu.make_async_remote_copy(
            src_ref=acc.at[g], dst_ref=acc_in.at[g], send_sem=xs.at[0], recv_sem=xr.at[g],
            device_id=(g, sec, ten), device_id_type=MESH).wait_recv()
        result = result + acc_in[g]
    hstage[...] = result.astype(jnp.bfloat16)
    store = pltpu.make_async_copy(hstage, head_out, loc.at[2])
    store.start()
    for k in range(1, n_dp):
        swap(k).wait_send()
    for c in range(tiles + 1):
        out_copy(c).wait()
    store.wait()


def per_device(mesh, sent_cot, saved_heads, out_proj):
    n_dp, n_sec, n_ten = (mesh.shape[a] for a in ("dp", "section", "tensor"))
    cot, heads, weight = sent_cot[0, 0], saved_heads[0, 0], out_proj[0]
    tokens, depth = cot.shape[1:]
    feats = weight.shape[1]
    extra = ROWS - tokens
    tiles = tokens // extra
    width = depth // n_dp // (tiles + 1)
    cut = cot.reshape(2, tokens, n_dp, tiles + 1, width).transpose(2, 0, 3, 1, 4)
    packed = jnp.concatenate(
        [cut[:, :, :tiles], cut[:, :, tiles].reshape(n_dp, 2, tiles, extra, width)], axis=3)
    count = n_ten * 2 * ROWS
    parts = ((0, 2), (2, 4), (4, 6), (6, 7)) if tiles == 7 else tuple((c, c + 1) for c in range(tiles))
    n_parts = len(parts)
    dims = (n_dp, n_sec, n_ten, tiles, width, tokens, parts)
    rows = depth // n_dp
    dma = pltpu.SemaphoreType.DMA
    head_out, proj = pl.pallas_call(
        functools.partial(kernel, dims),
        out_shape=(jax.ShapeDtypeStruct((count, feats), jnp.bfloat16),
                   jax.ShapeDtypeStruct((rows, feats), jnp.bfloat16)),
        in_specs=[pl.BlockSpec(memory_space=pl.ANY)] * 3,
        out_specs=(pl.BlockSpec(memory_space=pl.ANY),) * 2,
        scratch_shapes=[
            pltpu.VMEM((n_ten, n_dp, 2, tiles, ROWS, width), jnp.bfloat16),
            pltpu.VMEM((n_dp,) + heads.shape, jnp.bfloat16),
            pltpu.VMEM((count, feats), F32),
            pltpu.VMEM((n_dp, count, feats), jnp.bfloat16),
            pltpu.VMEM((n_dp, tiles, count, feats), jnp.bfloat16),
            pltpu.VMEM((rows, feats), jnp.bfloat16),
            pltpu.VMEM((rows, feats), jnp.bfloat16),
            pltpu.VMEM((rows, feats), F32),
            pltpu.VMEM((n_dp, count, feats), F32),
            pltpu.VMEM((n_dp, width, feats), F32),
            pltpu.VMEM((n_dp, count, feats), F32),
            pltpu.VMEM((count, feats), jnp.bfloat16),
            dma((n_dp, 2, n_parts)), dma((n_dp, 2, n_parts)),
            dma((2, n_ten, n_dp, n_parts)), dma((n_ten, n_dp, n_parts)),
            dma((n_dp,)), dma((n_dp,)), dma((n_dp,)), dma((n_dp,)),
            dma((3,)), dma((tiles + 1,)),
        ],
        compiler_params=pltpu.CompilerParams(
            collective_id=0, has_side_effects=True, vmem_limit_bytes=48 * 2**20),
        name="relay_grads",
    )(packed, heads, weight)
    head = head_out.reshape(n_ten, 2, ROWS, feats)[:, :, :tokens].transpose(1, 0, 2, 3)
    return head.reshape(1, 1, 2, n_ten * tokens, feats), proj[None]


def solution(mesh):
    return jax.shard_map(
        functools.partial(per_device, mesh),
        mesh=mesh,
        in_specs=(
            P("dp", "section", None, "tensor", None),
            P("dp", "section", None, None, "tensor"),
            P("section", None, "tensor"),
        ),
        out_specs=(P("dp", "section", None, None, "tensor"), P("section", "dp", "tensor")),
        check_vma=False,
    )
```

```python
import functools

import jax
import jax.numpy as jnp
from jax import lax
from jax.experimental import pallas as pl
from jax.experimental.pallas import tpu as pltpu
from jax.sharding import PartitionSpec as P

MESH = pl.DeviceIdType.MESH
F32 = jnp.float32
ROWS = 16


def kernel(dims, packed, heads, weight, head_out, proj_out,
           gath, hbuf, hwide, hfull, hspare, wbuf, stage, part, acc, spare, acc_in, lines, hstage,
           s1, r1, s2, r2, hs, hr, xs, xr, loc, outs):
    n_dp, n_sec, n_ten, tiles, width, tokens, parts = dims
    dp, sec, ten = (lax.axis_index(a) for a in ("dp", "section", "tensor"))
    spots = [(0, lax.rem(sec + n_sec - 1, n_sec)), (1, lax.rem(sec + 1, n_sec))]
    others = [lax.rem(dp + k, n_dp) for k in range(1, n_dp)]
    has_left, has_right = ten > 0, ten < n_ten - 1

    barrier = pltpu.get_barrier_semaphore()
    for h in range(n_dp):
        for _, place in spots:
            pl.semaphore_signal(barrier, inc=1, device_id=(h, place, ten), device_id_type=MESH)
    for h in others:
        pl.semaphore_signal(barrier, inc=1, device_id=(h, sec, ten), device_id_type=MESH)

    @pl.when(has_left)
    def _():
        pl.semaphore_signal(barrier, inc=1, device_id=(dp, sec, ten - 1), device_id_type=MESH)

    @pl.when(has_right)
    def _():
        pl.semaphore_signal(barrier, inc=1, device_id=(dp, sec, ten + 1), device_id_type=MESH)

    own_heads = pltpu.make_async_copy(heads, hbuf.at[dp], loc.at[0])
    own_heads.start()
    rows = width * (tiles + 1)
    load = pltpu.make_async_copy(weight.at[pl.ds(pl.multiple_of(dp * rows, rows), rows)], wbuf, loc.at[1])
    load.start()

    pl.semaphore_wait(barrier, 2 * n_dp + n_dp - 1 + jnp.where(has_left, 1, 0) + jnp.where(has_right, 1, 0))

    def first(k, r, m):
        low, high = parts[m]
        h = lax.rem(dp + k, n_dp)
        cut = pl.ds(low, high - low)
        return pltpu.make_async_remote_copy(
            src_ref=packed.at[h, r, cut], dst_ref=gath.at[ten, dp, r, cut],
            send_sem=s1.at[k, r, m], recv_sem=r1.at[dp, r, m],
            device_id=(h, spots[r][1], ten), device_id_type=MESH)

    def first_arrival(g, r, m):
        low, high = parts[m]
        cut = pl.ds(low, high - low)
        return pltpu.make_async_remote_copy(
            src_ref=packed.at[0, r, cut], dst_ref=gath.at[ten, g, r, cut],
            send_sem=s1.at[0, r, m], recv_sem=r1.at[g, r, m],
            device_id=(dp, spots[r][1], ten), device_id_type=MESH)

    def hop(item, g, m, step):
        low, high = parts[m]
        block = gath.at[item, g, :, pl.ds(low, high - low)]
        return pltpu.make_async_remote_copy(
            src_ref=block, dst_ref=block,
            send_sem=s2.at[(step + 1) // 2, item, g, m], recv_sem=r2.at[item, g, m],
            device_id=(dp, sec, ten + step), device_id_type=MESH)

    for m in range(len(parts)):
        for k in range(n_dp):
            for r in range(2):
                first(k, r, m).start()
    own_heads.wait()

    def head_copy(k):
        return pltpu.make_async_remote_copy(
            src_ref=heads, dst_ref=hbuf.at[dp],
            send_sem=hs.at[k - 1], recv_sem=hr.at[dp],
            device_id=(lax.rem(dp + k, n_dp), sec, ten), device_id_type=MESH)

    for k in range(1, n_dp):
        head_copy(k).start()

    for m in range(len(parts)):
        for k in range(n_dp):
            g = lax.rem(dp + k, n_dp)
            for r in range(2):
                first_arrival(g, r, m).wait_recv()

            @pl.when(has_right)
            def _():
                hop(ten, g, m, 1).start()

            @pl.when(has_left)
            def _():
                hop(ten, g, m, -1).start()

    for g in others:
        pltpu.make_async_remote_copy(
            src_ref=heads, dst_ref=hbuf.at[g], send_sem=hs.at[0], recv_sem=hr.at[g],
            device_id=(g, sec, ten), device_id_type=MESH).wait_recv()
    load.wait()
    count, feats = hwide.shape
    place = lax.rem(lax.broadcasted_iota(jnp.int32, (count, feats), 0), ROWS)
    length = n_ten * tokens
    extra = ROWS - tokens
    for g in range(n_dp):
        for r in range(2):
            rows_r = hbuf[g, r].astype(F32)
            for t in range(n_ten):
                turned = pltpu.roll(rows_r, length - t * tokens, 0) if t else rows_r
                at = (2 * t + r) * ROWS
                hwide[at:at + ROWS] = turned[:ROWS]
        wide = hwide[...]
        hfull[g] = jnp.where(place < tokens, wide, 0.0).astype(jnp.bfloat16)
        for c in range(tiles):
            turned = pltpu.roll(wide, tokens - extra * c, 0) if tokens - extra * c else wide
            hspare[g, c] = jnp.where(place >= tokens, turned, 0.0).astype(jnp.bfloat16)
        acc[g] = jnp.zeros(acc.shape[1:], F32)
        spare[g] = jnp.zeros(spare.shape[1:], F32)

    def out_copy(c):
        cut = pl.ds(c * width, width)
        return pltpu.make_async_copy(stage.at[cut], proj_out.at[cut], outs.at[c])

    def tile_term(g, c):
        block = gath[:, g, :, c].reshape(count, width)
        sides = jnp.concatenate([hfull[g], hspare[g, c]], axis=1)
        both = lax.dot_general(block, sides, (((0,), (0,)), ((), ())), preferred_element_type=F32)
        term = both[:, :feats]
        spare[g] += both[:, feats:]
        sides = jnp.concatenate(
            [wbuf[c * width:(c + 1) * width], wbuf[tiles * width:(tiles + 1) * width]], axis=1)
        both = jnp.dot(block, sides, preferred_element_type=F32)
        head, tail = both[:, :feats], both[:, feats:]
        back = count - (tokens - extra * c)
        tail = pltpu.roll(tail, back, 0) if back != count else tail
        mine = (place >= extra * c) & (place < extra * (c + 1))
        acc[g] += head + jnp.where(mine, tail, 0.0)
        return term.astype(jnp.bfloat16).astype(F32)

    def sum_others(terms):
        return functools.reduce(lambda a, b: a + b, terms)

    def pass_on(d, g, m):
        @pl.when(ten - d >= 0)
        def _():
            hop(ten - d, g, m, 1).wait_recv()

            @pl.when(has_right)
            def _():
                hop(ten - d, g, m, 1).start()

        @pl.when(ten + d < n_ten)
        def _():
            hop(ten + d, g, m, -1).wait_recv()

            @pl.when(has_left)
            def _():
                hop(ten + d, g, m, -1).start()

    def swap(k):
        g = lax.rem(dp + k, n_dp)
        return pltpu.make_async_remote_copy(
            src_ref=acc.at[g], dst_ref=acc_in.at[dp],
            send_sem=xs.at[k - 1], recv_sem=xr.at[dp],
            device_id=(g, sec, ten), device_id_type=MESH)

    def middle(d, carry):
        for g in others + [dp]:
            for m in range(len(parts)):
                pass_on(d, g, m)
        return carry

    lax.fori_loop(1, n_ten - 1, middle, 0)
    for m, (low, high) in enumerate(parts):
        for g in others:
            pass_on(n_ten - 1, g, m)
        for c in range(low, high):
            part[c * width:(c + 1) * width] = sum_others([tile_term(g, c) for g in others])
    for k in range(1, n_dp):
        swap(k).start()
    for m in range(len(parts)):
        for k in range(n_dp):
            for r in range(2):
                first(k, r, m).wait_send()
    for k in range(1, n_dp):
        head_copy(k).wait_send()

    def drain(item, carry):
        for m in range(len(parts)):
            for g in range(n_dp):
                @pl.when(has_right & (item <= ten))
                def _():
                    hop(item, g, m, 1).wait_send()

                @pl.when(has_left & (item >= ten))
                def _():
                    hop(item, g, m, -1).wait_send()
        return carry

    @pl.when(jnp.logical_not(has_left & has_right))
    def _():
        lax.fori_loop(0, n_ten, drain, 0)

    part[tiles * width:] = sum_others([spare[g].astype(jnp.bfloat16).astype(F32) for g in others])
    for m, (low, high) in enumerate(parts):
        pass_on(n_ten - 1, dp, m)
        for c in range(low, high):
            cut = slice(c * width, (c + 1) * width)
            stage[cut] = (part[cut] + tile_term(dp, c)).astype(jnp.bfloat16)
            out_copy(c).start()

    own = spare[dp].astype(jnp.bfloat16).astype(F32)
    stage[tiles * width:] = (part[tiles * width:] + own).astype(jnp.bfloat16)
    out_copy(tiles).start()

    @pl.when(has_left & has_right)
    def _():
        lax.fori_loop(0, n_ten, drain, 0)

    result = acc[dp]
    for g in others:
        pltpu.make_async_remote_copy(
            src_ref=acc.at[g], dst_ref=acc_in.at[g], send_sem=xs.at[0], recv_sem=xr.at[g],
            device_id=(g, sec, ten), device_id_type=MESH).wait_recv()
        result = result + acc_in[g]
    for r in range(2):
        for t in range(n_ten):
            at = (2 * t + r) * ROWS
            lines[r, t * tokens:t * tokens + ROWS] = result[at:at + ROWS]
        hstage[r] = lines[r, :length].astype(jnp.bfloat16)
    store = pltpu.make_async_copy(hstage, head_out, loc.at[2])
    store.start()
    for k in range(1, n_dp):
        swap(k).wait_send()
    for c in range(tiles + 1):
        out_copy(c).wait()
    store.wait()


def finish(pieces, head, proj, head_out, proj_out, sems):
    rows = proj.shape[0] // pieces
    copies = [pltpu.make_async_copy(head, head_out, sems.at[pieces])]
    for c in range(pieces):
        cut = pl.ds(c * rows, rows)
        copies.append(pltpu.make_async_copy(proj.at[cut], proj_out.at[cut], sems.at[c]))
    for copy in copies:
        copy.start()
    for copy in copies:
        copy.wait()


def per_device(mesh, sent_cot, saved_heads, out_proj):
    n_dp, n_sec, n_ten = (mesh.shape[a] for a in ("dp", "section", "tensor"))
    cot, heads, weight = sent_cot[0, 0], saved_heads[0, 0], out_proj[0]
    tokens, depth = cot.shape[1:]
    feats = weight.shape[1]
    extra = ROWS - tokens
    tiles = tokens // extra
    width = depth // n_dp // (tiles + 1)
    cut = cot.reshape(2, tokens, n_dp, tiles + 1, width).transpose(2, 0, 3, 1, 4)
    packed = jnp.concatenate(
        [cut[:, :, :tiles], cut[:, :, tiles].reshape(n_dp, 2, tiles, extra, width)], axis=3)
    count = n_ten * 2 * ROWS
    parts = ((0, 2), (2, 4), (4, 6), (6, 7)) if tiles == 7 else tuple((c, c + 1) for c in range(tiles))
    n_parts = len(parts)
    dims = (n_dp, n_sec, n_ten, tiles, width, tokens, parts)
    rows = depth // n_dp
    dma = pltpu.SemaphoreType.DMA
    head_out, proj = pl.pallas_call(
        functools.partial(kernel, dims),
        out_shape=(jax.ShapeDtypeStruct(heads.shape, jnp.bfloat16),
                   jax.ShapeDtypeStruct((rows, feats), jnp.bfloat16)),
        in_specs=[pl.BlockSpec(memory_space=pl.ANY)] * 3,
        out_specs=(pl.BlockSpec(memory_space=pl.ANY),) * 2,
        scratch_shapes=[
            pltpu.VMEM((n_ten, n_dp, 2, tiles, ROWS, width), jnp.bfloat16),
            pltpu.VMEM((n_dp,) + heads.shape, jnp.bfloat16),
            pltpu.VMEM((count, feats), F32),
            pltpu.VMEM((n_dp, count, feats), jnp.bfloat16),
            pltpu.VMEM((n_dp, tiles, count, feats), jnp.bfloat16),
            pltpu.VMEM((rows, feats), jnp.bfloat16),
            pltpu.VMEM((rows, feats), jnp.bfloat16),
            pltpu.VMEM((rows, feats), F32),
            pltpu.VMEM((n_dp, count, feats), F32),
            pltpu.VMEM((n_dp, width, feats), F32),
            pltpu.VMEM((n_dp, count, feats), F32),
            pltpu.VMEM((2, -(-(n_ten * tokens + extra) // 8) * 8, feats), F32),
            pltpu.VMEM(heads.shape, jnp.bfloat16),
            dma((n_dp, 2, n_parts)), dma((n_dp, 2, n_parts)),
            dma((2, n_ten, n_dp, n_parts)), dma((n_ten, n_dp, n_parts)),
            dma((n_dp,)), dma((n_dp,)), dma((n_dp,)), dma((n_dp,)),
            dma((3,)), dma((tiles + 1,)),
        ],
        compiler_params=pltpu.CompilerParams(
            collective_id=0, has_side_effects=True, vmem_limit_bytes=48 * 2**20),
        name="relay_grads",
    )(packed, heads, weight)
    head_out, proj = pl.pallas_call(
        functools.partial(finish, tiles + 1),
        out_shape=(jax.ShapeDtypeStruct(heads.shape, jnp.bfloat16),
                   jax.ShapeDtypeStruct((rows, feats), jnp.bfloat16)),
        in_specs=[pl.BlockSpec(memory_space=pl.ANY)] * 2,
        out_specs=(pl.BlockSpec(memory_space=pl.ANY),) * 2,
        scratch_shapes=[dma((tiles + 2,))],
        compiler_params=pltpu.CompilerParams(vmem_limit_bytes=2**20),
        name="write_out",
    )(head_out, proj)
    return head_out[None, None], proj[None]


def solution(mesh):
    return jax.shard_map(
        functools.partial(per_device, mesh),
        mesh=mesh,
        in_specs=(
            P("dp", "section", None, "tensor", None),
            P("dp", "section", None, None, "tensor"),
            P("section", None, "tensor"),
        ),
        out_specs=(P("dp", "section", None, None, "tensor"), P("section", "dp", "tensor")),
        check_vma=False,
    )
```

```python
import functools

import jax
import jax.numpy as jnp
from jax import lax
from jax.experimental import pallas as pl
from jax.experimental.pallas import tpu as pltpu
from jax.sharding import PartitionSpec as P

MESH = pl.DeviceIdType.MESH
F32 = jnp.float32
ROWS = 16


def kernel(dims, packed, heads, weight, head_out, proj_out,
           gath, hbuf, hwide, hfull, hspare, wbuf, stage, part, acc, spare, acc_in, lines, hstage,
           s1, r1, s2, r2, hs, hr, xs, xr, loc, outs):
    n_dp, n_sec, n_ten, tiles, width, tokens, parts = dims
    dp, sec, ten = (lax.axis_index(a) for a in ("dp", "section", "tensor"))
    spots = [(0, lax.rem(sec + n_sec - 1, n_sec)), (1, lax.rem(sec + 1, n_sec))]
    others = [lax.rem(dp + k, n_dp) for k in range(1, n_dp)]
    has_left, has_right = ten > 0, ten < n_ten - 1

    barrier = pltpu.get_barrier_semaphore()
    for h in range(n_dp):
        for _, place in spots:
            pl.semaphore_signal(barrier, inc=1, device_id=(h, place, ten), device_id_type=MESH)
    for h in others:
        pl.semaphore_signal(barrier, inc=1, device_id=(h, sec, ten), device_id_type=MESH)

    @pl.when(has_left)
    def _():
        pl.semaphore_signal(barrier, inc=1, device_id=(dp, sec, ten - 1), device_id_type=MESH)

    @pl.when(has_right)
    def _():
        pl.semaphore_signal(barrier, inc=1, device_id=(dp, sec, ten + 1), device_id_type=MESH)

    own_heads = pltpu.make_async_copy(heads, hbuf.at[dp], loc.at[0])
    own_heads.start()
    rows = width * (tiles + 1)
    load = pltpu.make_async_copy(weight.at[pl.ds(pl.multiple_of(dp * rows, rows), rows)], wbuf, loc.at[1])
    load.start()

    pl.semaphore_wait(barrier, 2 * n_dp + n_dp - 1 + jnp.where(has_left, 1, 0) + jnp.where(has_right, 1, 0))

    def first(k, r, m):
        low, high = parts[m]
        h = lax.rem(dp + k, n_dp)
        cut = pl.ds(low, high - low)
        return pltpu.make_async_remote_copy(
            src_ref=packed.at[h, r, cut], dst_ref=gath.at[ten, dp, r, cut],
            send_sem=s1.at[k, r, m], recv_sem=r1.at[dp, r, m],
            device_id=(h, spots[r][1], ten), device_id_type=MESH)

    def first_arrival(g, r, m):
        low, high = parts[m]
        cut = pl.ds(low, high - low)
        return pltpu.make_async_remote_copy(
            src_ref=packed.at[0, r, cut], dst_ref=gath.at[ten, g, r, cut],
            send_sem=s1.at[0, r, m], recv_sem=r1.at[g, r, m],
            device_id=(dp, spots[r][1], ten), device_id_type=MESH)

    def hop(item, g, m, step):
        low, high = parts[m]
        block = gath.at[item, g, :, pl.ds(low, high - low)]
        return pltpu.make_async_remote_copy(
            src_ref=block, dst_ref=block,
            send_sem=s2.at[(step + 1) // 2, item, g, m], recv_sem=r2.at[item, g, m],
            device_id=(dp, sec, ten + step), device_id_type=MESH)

    for m in range(len(parts)):
        for k in range(n_dp):
            for r in range(2):
                first(k, r, m).start()
    own_heads.wait()

    def head_copy(k):
        return pltpu.make_async_remote_copy(
            src_ref=heads, dst_ref=hbuf.at[dp],
            send_sem=hs.at[k - 1], recv_sem=hr.at[dp],
            device_id=(lax.rem(dp + k, n_dp), sec, ten), device_id_type=MESH)

    for k in range(1, n_dp):
        head_copy(k).start()

    for m in range(len(parts)):
        for k in range(n_dp):
            g = lax.rem(dp + k, n_dp)
            for r in range(2):
                first_arrival(g, r, m).wait_recv()

            @pl.when(has_right)
            def _():
                hop(ten, g, m, 1).start()

            @pl.when(has_left)
            def _():
                hop(ten, g, m, -1).start()

    for g in others:
        pltpu.make_async_remote_copy(
            src_ref=heads, dst_ref=hbuf.at[g], send_sem=hs.at[0], recv_sem=hr.at[g],
            device_id=(g, sec, ten), device_id_type=MESH).wait_recv()
    load.wait()
    count, feats = hwide.shape
    place = lax.rem(lax.broadcasted_iota(jnp.int32, (count, feats), 0), ROWS)
    length = n_ten * tokens
    extra = ROWS - tokens
    for g in range(n_dp):
        for r in range(2):
            rows_r = hbuf[g, r].astype(F32)
            for t in range(n_ten):
                turned = pltpu.roll(rows_r, length - t * tokens, 0) if t else rows_r
                at = (2 * t + r) * ROWS
                hwide[at:at + ROWS] = turned[:ROWS]
        wide = hwide[...]
        hfull[g] = jnp.where(place < tokens, wide, 0.0).astype(jnp.bfloat16)
        for c in range(tiles):
            turned = pltpu.roll(wide, tokens - extra * c, 0) if tokens - extra * c else wide
            hspare[g, c] = jnp.where(place >= tokens, turned, 0.0).astype(jnp.bfloat16)
        acc[g] = jnp.zeros(acc.shape[1:], F32)
        spare[g] = jnp.zeros(spare.shape[1:], F32)

    def out_copy(c):
        cut = pl.ds(c * width, width)
        return pltpu.make_async_copy(stage.at[cut], proj_out.at[cut], outs.at[c])

    def tile_term(g, c):
        block = gath[:, g, :, c].reshape(count, width)
        sides = jnp.concatenate([hfull[g], hspare[g, c]], axis=1)
        both = lax.dot_general(block, sides, (((0,), (0,)), ((), ())), preferred_element_type=F32)
        term = both[:, :feats]
        spare[g] += both[:, feats:]
        sides = jnp.concatenate(
            [wbuf[c * width:(c + 1) * width], wbuf[tiles * width:(tiles + 1) * width]], axis=1)
        both = jnp.dot(block, sides, preferred_element_type=F32)
        head, tail = both[:, :feats], both[:, feats:]
        back = count - (tokens - extra * c)
        tail = pltpu.roll(tail, back, 0) if back != count else tail
        mine = (place >= extra * c) & (place < extra * (c + 1))
        acc[g] += head + jnp.where(mine, tail, 0.0)
        return term.astype(jnp.bfloat16).astype(F32)

    def sum_others(terms):
        return functools.reduce(lambda a, b: a + b, terms)

    def pass_on(d, g, m):
        @pl.when(ten - d >= 0)
        def _():
            hop(ten - d, g, m, 1).wait_recv()

            @pl.when(has_right)
            def _():
                hop(ten - d, g, m, 1).start()

        @pl.when(ten + d < n_ten)
        def _():
            hop(ten + d, g, m, -1).wait_recv()

            @pl.when(has_left)
            def _():
                hop(ten + d, g, m, -1).start()

    def swap(k):
        g = lax.rem(dp + k, n_dp)
        return pltpu.make_async_remote_copy(
            src_ref=acc.at[g], dst_ref=acc_in.at[dp],
            send_sem=xs.at[k - 1], recv_sem=xr.at[dp],
            device_id=(g, sec, ten), device_id_type=MESH)

    def middle(d, carry):
        for g in others + [dp]:
            for m in range(len(parts)):
                pass_on(d, g, m)
        return carry

    lax.fori_loop(1, n_ten - 1, middle, 0)
    for m, (low, high) in enumerate(parts):
        for g in others:
            pass_on(n_ten - 1, g, m)
        for c in range(low, high):
            part[c * width:(c + 1) * width] = sum_others([tile_term(g, c) for g in others])
    for k in range(1, n_dp):
        swap(k).start()
    for m in range(len(parts)):
        for k in range(n_dp):
            for r in range(2):
                first(k, r, m).wait_send()
    for k in range(1, n_dp):
        head_copy(k).wait_send()

    def drain(item, carry):
        for m in range(len(parts)):
            for g in range(n_dp):
                @pl.when(has_right & (item <= ten))
                def _():
                    hop(item, g, m, 1).wait_send()

                @pl.when(has_left & (item >= ten))
                def _():
                    hop(item, g, m, -1).wait_send()
        return carry

    @pl.when(jnp.logical_not(has_left & has_right))
    def _():
        lax.fori_loop(0, n_ten, drain, 0)

    part[tiles * width:] = sum_others([spare[g].astype(jnp.bfloat16).astype(F32) for g in others])
    for m, (low, high) in enumerate(parts):
        pass_on(n_ten - 1, dp, m)
        for c in range(low, high):
            cut = slice(c * width, (c + 1) * width)
            stage[cut] = (part[cut] + tile_term(dp, c)).astype(jnp.bfloat16)
            out_copy(c).start()

    own = spare[dp].astype(jnp.bfloat16).astype(F32)
    stage[tiles * width:] = (part[tiles * width:] + own).astype(jnp.bfloat16)
    out_copy(tiles).start()

    @pl.when(has_left & has_right)
    def _():
        lax.fori_loop(0, n_ten, drain, 0)

    result = acc[dp]
    for g in others:
        pltpu.make_async_remote_copy(
            src_ref=acc.at[g], dst_ref=acc_in.at[g], send_sem=xs.at[0], recv_sem=xr.at[g],
            device_id=(g, sec, ten), device_id_type=MESH).wait_recv()
        result = result + acc_in[g]
    for r in range(2):
        for t in range(n_ten):
            at = (2 * t + r) * ROWS
            lines[r, t * tokens:t * tokens + ROWS] = result[at:at + ROWS]
        hstage[r] = lines[r, :length].astype(jnp.bfloat16)
    store = pltpu.make_async_copy(hstage, head_out, loc.at[2])
    store.start()
    for k in range(1, n_dp):
        swap(k).wait_send()
    for c in range(tiles + 1):
        out_copy(c).wait()
    store.wait()


def finish(pieces, head, proj, head_out, proj_out, sems):
    rows = proj.shape[0] // pieces
    copies = [pltpu.make_async_copy(head, head_out, sems.at[pieces])]
    for c in range(pieces):
        cut = pl.ds(c * rows, rows)
        copies.append(pltpu.make_async_copy(proj.at[cut], proj_out.at[cut], sems.at[c]))
    for copy in copies:
        copy.start()
    for copy in copies:
        copy.wait()


def per_device(mesh, sent_cot, saved_heads, out_proj):
    n_dp, n_sec, n_ten = (mesh.shape[a] for a in ("dp", "section", "tensor"))
    cot, heads, weight = sent_cot[0, 0], saved_heads[0, 0], out_proj[0]
    tokens, depth = cot.shape[1:]
    feats = weight.shape[1]
    extra = ROWS - tokens
    tiles = tokens // extra
    width = depth // n_dp // (tiles + 1)
    cut = cot.reshape(2, tokens, n_dp, tiles + 1, width).transpose(2, 0, 3, 1, 4)
    packed = jnp.concatenate(
        [cut[:, :, :tiles], cut[:, :, tiles].reshape(n_dp, 2, tiles, extra, width)], axis=3)
    count = n_ten * 2 * ROWS
    parts = ((0, 2), (2, 4), (4, 6), (6, 7)) if tiles == 7 else tuple((c, c + 1) for c in range(tiles))
    n_parts = len(parts)
    dims = (n_dp, n_sec, n_ten, tiles, width, tokens, parts)
    rows = depth // n_dp
    dma = pltpu.SemaphoreType.DMA
    head_out, proj = pl.pallas_call(
        functools.partial(kernel, dims),
        out_shape=(jax.ShapeDtypeStruct(heads.shape, jnp.bfloat16),
                   jax.ShapeDtypeStruct((rows, feats), jnp.bfloat16)),
        in_specs=[pl.BlockSpec(memory_space=pl.ANY)] * 3,
        out_specs=(pl.BlockSpec(memory_space=pl.ANY),) * 2,
        scratch_shapes=[
            pltpu.VMEM((n_ten, n_dp, 2, tiles, ROWS, width), jnp.bfloat16),
            pltpu.VMEM((n_dp,) + heads.shape, jnp.bfloat16),
            pltpu.VMEM((count, feats), F32),
            pltpu.VMEM((n_dp, count, feats), jnp.bfloat16),
            pltpu.VMEM((n_dp, tiles, count, feats), jnp.bfloat16),
            pltpu.VMEM((rows, feats), jnp.bfloat16),
            pltpu.VMEM((rows, feats), jnp.bfloat16),
            pltpu.VMEM((rows, feats), F32),
            pltpu.VMEM((n_dp, count, feats), F32),
            pltpu.VMEM((n_dp, width, feats), F32),
            pltpu.VMEM((n_dp, count, feats), F32),
            pltpu.VMEM((2, -(-(n_ten * tokens + extra) // 8) * 8, feats), F32),
            pltpu.VMEM(heads.shape, jnp.bfloat16),
            dma((n_dp, 2, n_parts)), dma((n_dp, 2, n_parts)),
            dma((2, n_ten, n_dp, n_parts)), dma((n_ten, n_dp, n_parts)),
            dma((n_dp,)), dma((n_dp,)), dma((n_dp,)), dma((n_dp,)),
            dma((3,)), dma((tiles + 1,)),
        ],
        compiler_params=pltpu.CompilerParams(
            collective_id=0, has_side_effects=True, vmem_limit_bytes=48 * 2**20),
        name="relay_grads",
    )(packed, heads, weight)
    head_out, proj = pl.pallas_call(
        functools.partial(finish, 2),
        out_shape=(jax.ShapeDtypeStruct(heads.shape, jnp.bfloat16),
                   jax.ShapeDtypeStruct((rows, feats), jnp.bfloat16)),
        in_specs=[pl.BlockSpec(memory_space=pl.ANY)] * 2,
        out_specs=(pl.BlockSpec(memory_space=pl.ANY),) * 2,
        scratch_shapes=[dma((2 + 1,))],
        compiler_params=pltpu.CompilerParams(vmem_limit_bytes=2**20),
        name="write_out",
    )(head_out, proj)
    return head_out[None, None], proj[None]


def solution(mesh):
    return jax.shard_map(
        functools.partial(per_device, mesh),
        mesh=mesh,
        in_specs=(
            P("dp", "section", None, "tensor", None),
            P("dp", "section", None, None, "tensor"),
            P("section", None, "tensor"),
        ),
        out_specs=(P("dp", "section", None, None, "tensor"), P("section", "dp", "tensor")),
        check_vma=False,
    )
```
